512 devices in a mesh: chan: 128 (over x, z, y_hi), tm: 4 (over y_lo, core).
Axes of the slice: x: 4, y: 4 (y_hi: 2, y_lo: 2; y = y_hi * 2 + y_lo), z: 16, core: 2. Of those that a mesh axis runs over, the one named last changes fastest.
Arguments:
- spectra: bfloat16 [256, 10240, 128], P('tm', 'chan'), may hold values from -150 to 150
- live_mask: int32 [10240], P('chan'), may hold values 0 or 1
Outputs:
- correlations: bfloat16 [2, 80, 10240, 128], P(None, 'tm', 'chan')
The draws below stay inside these ranges and needn't reach their ends.
All inputs are finite; a program needn't handle non-finite values. No bound on the sum of `live_mask` on one device may be relied on, other than what follows from the above.
Results may differ from the reference program's by a relative error of at most 0.015.
Values may be sent and summed in bfloat16 or wider, within the bound.
A program may use at most 64 MiB of HBM per device.

```python
import math
import jax
import jax.numpy as jnp
from jax import lax

CHAN_DEV = 80
WIN_DEV = 64
F = 64
ROUNDS = 2
CHANNELS = 10240
WINDOWS = 256
N_CHAN = 128
N_TM = 4


def draw_spectra(key, part):
    first, second, third = jax.random.split(key, 3)
    shape = (WINDOWS, CHANNELS, 2 * F)
    base = jnp.clip(jax.random.normal(first, shape, jnp.float32), -6.0, 6.0)
    scales = jnp.exp(jax.random.uniform(second, (WINDOWS, CHANNELS, 1), jnp.float32, math.log(0.1), math.log(10.0)))
    colour = jnp.exp(jax.random.uniform(third, (1, CHANNELS, 2 * F), jnp.float32, -0.7, 0.7))
    return (base * scales * colour).astype(jnp.bfloat16)


def plant(array, stream_key, low, top_value):
    place = [jax.random.randint(jax.random.fold_in(stream_key, axis), (), 0, length) for axis, length in enumerate(array.shape)]
    longest = array.shape.index(max(array.shape))
    next_to = place[:longest] + [(place[longest] + 1) % array.shape[longest]] + place[longest + 1:]
    return array.at[tuple(place)].set(low).at[tuple(next_to)].set(top_value)


def setup_inputs(seed: int = 0) -> dict:
    seeds = jax.random.split(jax.random.key(seed), 3)
    return {
        "spectra": draw_spectra(jax.random.fold_in(seeds[2], 71), 0),
        "live_mask": plant((jax.random.randint(seeds[1], (CHANNELS,), 0, 8) < 7).astype(jnp.int32), jax.random.fold_in(seeds[1], 1), 0, 1),
    }


def lag_table(frequency, windows_all):
    bins = jnp.arange(frequency).astype(jnp.float32)
    shifts = (jnp.arange(2 * frequency) - frequency).astype(jnp.float32)
    phase = 2.0 * math.pi / (2 * frequency) * bins[:, None] * shifts[None, :]
    weight = jnp.where(bins == 0, 1.0, 2.0).astype(jnp.float32)
    scaling = 1.0 / (2.0 * math.sqrt(frequency * windows_all))
    upper = weight[:, None] * jnp.cos(phase) * scaling
    lower = -weight[:, None] * jnp.sin(phase) * scaling
    return jnp.concatenate([upper, lower], axis=0).astype(jnp.float32)

def whiten(spectra, live_mask):
    values = spectra.astype(jnp.float32)
    mean_square = lax.optimization_barrier(jnp.mean(values * values, axis=-1, keepdims=True))
    gated = values * live_mask.astype(jnp.float32)[None, :, None]
    return (gated * lax.rsqrt(mean_square + 1e-06)).astype(jnp.bfloat16)

def cross(own_block, other_block):
    half = own_block.shape[-1] // 2
    own_real, own_imag = (own_block[..., :half], own_block[..., half:])
    other_real, other_imag = (other_block[..., :half], other_block[..., half:])
    real_part = jnp.einsum('wjf,wif->jif', other_real, own_real) + jnp.einsum('wjf,wif->jif', other_imag, own_imag)
    imag_part = jnp.einsum('wjf,wif->jif', other_real, own_imag) - jnp.einsum('wjf,wif->jif', other_imag, own_real)
    return jnp.concatenate([real_part, imag_part], axis=-1)

def reference(spectra, live_mask):
    white = whiten(spectra, live_mask)
    blocks = white.reshape(N_TM, WIN_DEV, N_CHAN, CHAN_DEV, 2 * F).transpose(2, 0, 1, 3, 4)
    lag_matrix = lag_table(F, WINDOWS)
    results = []
    for offset in range(1, ROUNDS + 1):
        partner = jnp.roll(blocks, -offset, axis=0)

        def per_block(block_pair):
            own_block, other_block = block_pair
            stacked = jnp.zeros((CHAN_DEV, CHAN_DEV, 2 * F), jnp.float32)
            for quarter in range(N_TM):
                term = cross(own_block[quarter].astype(jnp.float32), other_block[quarter].astype(jnp.float32))
                rounded = lax.optimization_barrier(term.astype(jnp.bfloat16))
                stacked = stacked + rounded.astype(jnp.float32)
            lagged = jnp.dot(stacked.reshape(-1, 2 * F), lag_matrix, precision=lax.Precision.HIGHEST)
            return lagged.reshape(CHAN_DEV, CHAN_DEV, 2 * F).astype(jnp.bfloat16)
        per_pair = lax.map(per_block, (blocks, partner))
        results.append(per_pair.transpose(1, 0, 2, 3).reshape(CHAN_DEV, CHANNELS, 2 * F))
    return jnp.stack(results)
```

```python
import functools
import math

import jax
import jax.numpy as jnp
import ml_dtypes
import numpy as np
from jax import lax
from jax.experimental import pallas as pl
from jax.experimental.pallas import tpu as pltpu
from jax.sharding import PartitionSpec as P

MESH = pl.DeviceIdType.MESH
F32, BF16 = jnp.float32, jnp.bfloat16
PLANES = 64
SLOTS = 8
CH = 80
WIN = 64
LANES = 128
GROUPS = 4
ROWS = 112
DOWN, UP = 0, 1
DIRECTION = (DOWN, DOWN, DOWN, DOWN)


def lag_tables(windows_all):
    bins = np.arange(64)
    shifts = np.arange(128) - 64
    phase = 2.0 * np.pi / 128 * bins[:, None] * shifts[None, :]
    weight = np.where(bins == 0, 1.0, 2.0)
    scaling = 1.0 / (2.0 * math.sqrt(64 * windows_all))
    parts = np.stack([weight[:, None] * np.cos(phase), -weight[:, None] * np.sin(phase)]) * scaling
    parts = parts.reshape(2, SLOTS, GROUPS, 2, LANES)
    main = parts.transpose(0, 3, 2, 1, 4).reshape(LANES, LANES)
    rest = parts.transpose(3, 0, 2, 1, 4).reshape(LANES, LANES)
    return np.stack([main, rest]).astype(ml_dtypes.bfloat16)


def flip(slot, bits):
    for bit in range(3):
        if bits >> bit & 1:
            step = 1 << bit
            slot = slot + step - 2 * step * ((slot // step) % 2)
    return slot


def device(plane, slot):
    plane = (plane + PLANES) % PLANES
    return (plane * 2 + slot // 4, slot % 4)


def kernel(x_ref, mask_ref, lag_ref, out_ref, xf, tf, sent, own, other, made, got, gotf,
           send_a, recv_a, send_z, recv_z, send_r, recv_r, local):
    plane = lax.axis_index("chan") // 2
    quarter = lax.axis_index("tm")
    slot = (lax.axis_index("chan") % 2) * 4 + quarter
    any_up = UP in DIRECTION

    barrier = pltpu.get_barrier_semaphore()
    greeted = [device(plane, flip(slot, k)) for k in range(1, SLOTS)]
    for step in (-1, 1):
        greeted += [device(plane + step, flip(slot, k)) for k in range(SLOTS if any_up else 1)]
    for target in greeted:
        pl.semaphore_signal(barrier, inc=1, device_id=target, device_id_type=MESH)

    lane = lax.broadcasted_iota(jnp.int32, (64, LANES), 1)
    low = lane < 64

    def widen(n, carry):
        rows = pl.ds(pl.multiple_of(n * 128, 128), 128)
        xf[rows, :] = x_ref[rows, :].astype(F32)
        return carry

    lax.fori_loop(0, WIN * CH // 128, widen, 0)

    def turn(channel, place):
        pair = [xf[pl.ds(channel + k, WIN, stride=CH), :] for k in range(2)]
        z = jnp.concatenate(pair, axis=0).T
        power = jnp.sum(z * z, axis=0, keepdims=True) * (1.0 / LANES)
        live0 = mask_ref[channel].astype(F32)
        live1 = mask_ref[channel + 1].astype(F32)
        z = z * (lax.rsqrt(power + 1e-6) * jnp.where(low[:1], live0, live1))
        top, bottom = z[:64], z[64:]
        tf[pl.ds(place, 64, stride=CH), :] = jnp.where(low, top, pltpu.roll(bottom, 64, 1))
        tf[pl.ds(place + 1, 64, stride=CH), :] = jnp.where(low, pltpu.roll(top, 64, 1), bottom)

    def turn_first(n, carry):
        turn(20 * (n // 8) + 2 * (n % 8), 2 * n)
        return carry

    def turn_rest(n, carry):
        turn(20 * (n // 2) + 16 + 2 * (n % 2), 64 + 2 * n)
        return carry

    lax.fori_loop(0, 32, turn_first, 0)
    lax.fori_loop(0, 8, turn_rest, 0)

    def exchange(g, k):
        peer = flip(slot, k)
        return pltpu.make_async_remote_copy(
            src_ref=sent.at[peer, g], dst_ref=own.at[g, slot],
            send_sem=send_a.at[g, k], recv_sem=recv_a.at[g, k],
            device_id=device(plane, peer), device_id_type=MESH)

    def keep(g):
        return pltpu.make_async_copy(sent.at[slot, g], own.at[g, slot], local.at[g])

    for g in range(GROUPS):
        def narrow(d, carry, g=g):
            for ff in range(2):
                row = pl.multiple_of((d * 8 + g * 2 + ff) * CH, 16)
                sent[d, g, ff] = tf[pl.ds(row, CH), :].astype(BF16)
            return carry

        lax.fori_loop(0, SLOTS, narrow, 0)
        if g == 0:
            pl.semaphore_wait(barrier, len(greeted))
        for k in (4, 5, 6, 7, 2, 3, 1):
            exchange(g, k).start()
        keep(g).start()

    def forward(g):
        step = -1 if DIRECTION[g] == DOWN else 1
        return pltpu.make_async_remote_copy(
            src_ref=own.at[g], dst_ref=other.at[g], send_sem=send_z.at[g], recv_sem=recv_z.at[g],
            device_id=device(plane + step, slot), device_id_type=MESH)

    for g in range(GROUPS):
        keep(g).wait()
        for k in range(1, SLOTS):
            exchange(g, k).wait_recv()
        forward(g).start()

    sign = jnp.where(low[:1], 1.0, -1.0).astype(F32)
    piece = lax.broadcasted_iota(jnp.int32, (CH, LANES), 1) // 32

    def block(ref, g, which, ff):
        return jnp.concatenate([ref[g, which * 4 + q, ff] for q in range(4)], axis=1)

    def crossed(ref, g, which, ff):
        parts = [pltpu.roll(ref[g, which * 4 + q, ff].astype(F32), 64, 1) * sign for q in range(4)]
        return jnp.concatenate(parts, axis=1).astype(BF16)

    def cross(g):
        lower, upper = (own, other) if DIRECTION[g] == DOWN else (other, own)
        for b in range(2):
            left, rest = [], []
            for ff in range(2):
                plain, turned = block(lower, g, b, ff), crossed(lower, g, b, ff)
                tail = [plain[64:], turned[64:]]
                weights = jnp.concatenate([plain[:64], turned[:64]] + tail * 4, axis=0)
                first = block(lower, g, 1, ff) if b == 0 else block(upper, g, 0, ff)
                second = block(upper, g, b, ff)
                streamed = jnp.concatenate([first, second], axis=0)
                product = lax.dot_general(streamed, weights, (((1,), (1,)), ((), ())),
                                          preferred_element_type=F32)
                for r in range(2):
                    part = product[r * CH:(r + 1) * CH]
                    for t in range(4):
                        made[g, b * 4 + t, pl.ds(ff * 32 + r * 16, 16), :] = (
                            part[t * 16:(t + 1) * 16, :LANES].astype(BF16))
                    left.append(part[64:, :LANES])
                    rest.append(part[:, LANES:])
            edge = jnp.where(piece < 2, jnp.where(piece < 1, rest[0], rest[1]),
                             jnp.where(piece < 3, rest[2], rest[3])).astype(BF16)
            for t in range(4):
                fours = jnp.concatenate([a[t * 4:(t + 1) * 4] for a in left], axis=0)
                made[g, b * 4 + t, pl.ds(64, 16), :] = fours.astype(BF16)
                made[g, b * 4 + t, pl.ds(80, 16), :] = edge[t * 16:(t + 1) * 16]
                made[g, b * 4 + t, pl.ds(96, 16), :] = edge[64:]

    def deliver(g, k):
        owner = flip(slot, k)
        step = 0 if DIRECTION[g] == DOWN else -1
        return pltpu.make_async_remote_copy(
            src_ref=made.at[g, owner], dst_ref=got.at[g, slot],
            send_sem=send_r.at[g, k], recv_sem=recv_r.at[g, k],
            device_id=device(plane + step, owner), device_id_type=MESH)

    def retain(g):
        return pltpu.make_async_copy(made.at[g, slot], got.at[g, slot], local.at[GROUPS + g])

    for g in range(GROUPS):
        forward(g).wait_recv()
        cross(g)
        if DIRECTION[g] == DOWN:
            retain(g).start()
        for k in (4, 5, 6, 7, 2, 3, 1) + ((0,) if DIRECTION[g] == UP else ()):
            deliver(g, k).start()

    for g in range(GROUPS):
        if DIRECTION[g] == DOWN:
            retain(g).wait()
        for k in range(0 if DIRECTION[g] == UP else 1, SLOTS):
            deliver(g, k).wait_recv()

        def spread(d, carry, g=g):
            row = pl.multiple_of((g * SLOTS + d) * ROWS, 16)
            gotf[pl.ds(row, ROWS), :] = got[g, d].astype(F32)
            return carry

        lax.fori_loop(0, SLOTS, spread, 0)

    sources = GROUPS * SLOTS
    low16 = lax.broadcasted_iota(jnp.int32, (16, LANES), 1) // 32

    def rows_of(row):
        return gotf[pl.ds(row, sources, stride=ROWS), :]

    def lags(first, row_main, row_edge, stride_ff, stride_r):
        z = jnp.concatenate([rows_of(row_edge + j) for j in range(4)], axis=0).T
        pieces = []
        for j in range(4):
            for r in range(2):
                total = None
                for ff in range(2):
                    for c in range(2):
                        at = (ff * 4 + r * 2 + c) * 16
                        to = ff * 2 + c
                        moved = z[at:at + 16]
                        if (to - j) % 4:
                            moved = pltpu.roll(moved, ((to - j) % 4) * 32, 1)
                        total = moved if total is None else jnp.where(low16 == to, moved, total)
                pieces.append(total)
        edge = jnp.dot(jnp.concatenate(pieces, axis=0).astype(BF16), lag_ref[1], preferred_element_type=F32)
        for r in range(2):
            for half in range(2):
                rows = []
                for j in (2 * half, 2 * half + 1):
                    for ff in range(2):
                        rows.append(rows_of(row_main + ff * stride_ff + r * stride_r + j))
                z = jnp.concatenate(rows, axis=0).T
                top, bottom = z[:64], z[64:]
                lhs = jnp.concatenate([jnp.where(low, top, pltpu.roll(bottom, 64, 1)),
                                       jnp.where(low, pltpu.roll(top, 64, 1), bottom)], axis=0)
                body = jnp.dot(lhs.astype(BF16), lag_ref[0], preferred_element_type=F32)
                for n in range(2):
                    j = 2 * half + n
                    at = (j * 2 + r) * 16
                    pieces = []
                    for t in range(4):
                        pieces.append(body[n * 64 + t * 16:n * 64 + (t + 1) * 16])
                        pieces.append(edge[at + t * 4:at + (t + 1) * 4])
                    out_ref[r, first + j] = jnp.concatenate(pieces, axis=0).astype(BF16)

    def lags_first(n, carry):
        lags(4 * n, 4 * n, 80 + 4 * n, 32, 16)
        return carry

    lax.fori_loop(0, 4, lags_first, 0)
    lags(16, 64, 96 + 4 * quarter, 8, 4)

    for g in range(GROUPS):
        for k in range(1, SLOTS):
            exchange(g, k).wait_send()
        forward(g).wait_send()
        for k in range(0 if DIRECTION[g] == UP else 1, SLOTS):
            deliver(g, k).wait_send()


def shards(spectra, live_mask):
    windows = spectra.shape[0] * lax.axis_size("tm")
    tables = jnp.asarray(lag_tables(windows))
    vmem = pl.BlockSpec(memory_space=pltpu.VMEM)
    dma = pltpu.SemaphoreType.DMA
    return pl.pallas_call(
        kernel,
        out_shape=jax.ShapeDtypeStruct((2, 20, CH, LANES), BF16),
        in_specs=[vmem, pl.BlockSpec(memory_space=pltpu.SMEM), vmem],
        out_specs=vmem,
        scratch_shapes=[
            pltpu.VMEM((WIN * CH, LANES), F32),
            pltpu.VMEM((64 * CH, LANES), F32),
            pltpu.VMEM((SLOTS, GROUPS, 2, CH, LANES), BF16),
            pltpu.VMEM((GROUPS, SLOTS, 2, CH, LANES), BF16),
            pltpu.VMEM((GROUPS, SLOTS, 2, CH, LANES), BF16),
            pltpu.VMEM((GROUPS, SLOTS, ROWS, LANES), BF16),
            pltpu.VMEM((GROUPS, SLOTS, ROWS, LANES), BF16),
            pltpu.VMEM((GROUPS * SLOTS * ROWS, LANES), F32),
            dma((GROUPS, SLOTS)), dma((GROUPS, SLOTS)),
            dma((GROUPS,)), dma((GROUPS,)),
            dma((GROUPS, SLOTS)), dma((GROUPS, SLOTS)),
            dma((2 * GROUPS,)),
        ],
        compiler_params=pltpu.CompilerParams(
            collective_id=0, has_side_effects=True, vmem_limit_bytes=40 * 2**20),
        name="correlate",
    )(spectra.reshape(WIN * CH, LANES), live_mask, tables)


def solution(mesh):
    placed = (P("tm", "chan", None), P("chan"))
    return jax.shard_map(
        shards, mesh=mesh, in_specs=placed, out_specs=P(None, "tm", "chan", None), check_vma=False
    )
```

```python
import functools
import math

import jax
import jax.numpy as jnp
import ml_dtypes
import numpy as np
from jax import lax
from jax.experimental import pallas as pl
from jax.experimental.pallas import tpu as pltpu
from jax.sharding import PartitionSpec as P

MESH = pl.DeviceIdType.MESH
F32, BF16 = jnp.float32, jnp.bfloat16
PLANES = 64
SLOTS = 8
CH = 80
WIN = 64
LANES = 128
GROUPS = 4
ROWS = 112
DOWN, UP = 0, 1
DIRECTION = (DOWN, UP, DOWN, DOWN)
CHUNK = 16
NEAR_FIRST = (1, 2, 3, 6, 7, 4, 5)
FAR_FIRST = (4, 5, 6, 7, 2, 3, 1)


def lag_tables(windows_all):
    bins = np.arange(64)
    shifts = np.arange(128) - 64
    phase = 2.0 * np.pi / 128 * bins[:, None] * shifts[None, :]
    weight = np.where(bins == 0, 1.0, 2.0)
    scaling = 1.0 / (2.0 * math.sqrt(64 * windows_all))
    parts = np.stack([weight[:, None] * np.cos(phase), -weight[:, None] * np.sin(phase)]) * scaling
    parts = parts.reshape(2, SLOTS, GROUPS, 2, LANES)
    main = parts.transpose(0, 3, 2, 1, 4).reshape(LANES, LANES)
    rest = parts.transpose(3, 0, 2, 1, 4).reshape(LANES, LANES)
    return np.stack([main, rest]).astype(ml_dtypes.bfloat16)


def flip(slot, bits):
    for bit in range(3):
        if bits >> bit & 1:
            step = 1 << bit
            slot = slot + step - 2 * step * ((slot // step) % 2)
    return slot


def device(plane, slot):
    plane = (plane + PLANES) % PLANES
    return (plane * 2 + slot // 4, slot % 4)


def kernel(x_hbm, mask_hbm, lag_hbm, out_ref, x_ref, mask_ref, lag_ref, xf, tf, sent, own, other, made, got, gotf,
           send_a, recv_a, send_z, recv_z, send_r, recv_r, local, load):
    plane = lax.axis_index("chan") // 2
    quarter = lax.axis_index("tm")
    slot = (lax.axis_index("chan") % 2) * 4 + quarter
    any_up = UP in DIRECTION

    def fetch(n):
        part = (slice(None), pl.ds(pl.multiple_of(n * CHUNK, CHUNK), CHUNK), slice(None))
        return pltpu.make_async_copy(x_hbm.at[part], x_ref.at[part], load.at[n])

    chunks = CH // CHUNK
    fetch_mask = pltpu.make_async_copy(mask_hbm, mask_ref, load.at[chunks])
    fetch_lag = pltpu.make_async_copy(lag_hbm, lag_ref, load.at[chunks + 1])
    fetch_mask.start()
    for n in range(chunks):
        fetch(n).start()
    fetch_lag.start()

    barrier = pltpu.get_barrier_semaphore()
    greeted = [device(plane, flip(slot, k)) for k in range(1, SLOTS)]
    for step in (-1, 1):
        greeted += [device(plane + step, flip(slot, k)) for k in range(SLOTS if any_up else 1)]
    for target in greeted:
        pl.semaphore_signal(barrier, inc=1, device_id=target, device_id_type=MESH)

    lane = lax.broadcasted_iota(jnp.int32, (64, LANES), 1)
    low = lane < 64

    def turn(channel):
        t, m = channel // 20, channel % 20
        place = 16 * t + m + (m // 16) * (48 - 12 * t)
        pair = [xf[pl.ds(channel + k, WIN, stride=CH), :] for k in range(2)]
        z = jnp.concatenate(pair, axis=0).astype(BF16).T.astype(F32)
        power = jnp.sum(z * z, axis=0, keepdims=True) * (1.0 / LANES)
        live0 = mask_ref[channel].astype(F32)
        live1 = mask_ref[channel + 1].astype(F32)
        z = z * (lax.rsqrt(power + 1e-6) * jnp.where(low[:1], live0, live1))
        top, bottom = z[:64], z[64:]
        tf[pl.ds(place, 64, stride=CH), :] = jnp.where(low, top, pltpu.roll(bottom, 64, 1))
        tf[pl.ds(place + 1, 64, stride=CH), :] = jnp.where(low, pltpu.roll(top, 64, 1), bottom)

    def prepare(n, carry):
        fetch(n).wait()
        first = pl.multiple_of(n * CHUNK, CHUNK)

        def widen(w, c):
            for k in range(8):
                row = pl.multiple_of((w * 8 + k) * CH + first, CHUNK)
                xf[pl.ds(row, CHUNK), :] = x_ref[w * 8 + k, pl.ds(first, CHUNK), :].astype(F32)
            return c

        lax.fori_loop(0, WIN // 8, widen, 0)
        for k in range(0, CHUNK, 2):
            turn(first + k)
        return carry

    fetch_mask.wait()
    lax.fori_loop(0, chunks, prepare, 0)

    def exchange(g, k):
        peer = flip(slot, k)
        return pltpu.make_async_remote_copy(
            src_ref=sent.at[peer, g], dst_ref=own.at[g, slot],
            send_sem=send_a.at[g, k], recv_sem=recv_a.at[g, k],
            device_id=device(plane, peer), device_id_type=MESH)

    def keep(g):
        return pltpu.make_async_copy(sent.at[slot, g], own.at[g, slot], local.at[g])

    def forward(g, k):
        step = -1 if DIRECTION[g] == DOWN else 1
        source = flip(slot, k)
        return pltpu.make_async_remote_copy(
            src_ref=own.at[g, source] if k else sent.at[slot, g], dst_ref=other.at[g, source],
            send_sem=send_z.at[g, k], recv_sem=recv_z.at[g, k],
            device_id=device(plane + step, slot), device_id_type=MESH)

    for g in range(GROUPS):
        def narrow(d, carry, g=g):
            for ff in range(2):
                row = pl.multiple_of((d * 8 + g * 2 + ff) * CH, 16)
                sent[d, g, ff] = tf[pl.ds(row, CH), :].astype(BF16)
            return carry

        lax.fori_loop(0, SLOTS, narrow, 0)
        if g == 0:
            pl.semaphore_wait(barrier, len(greeted))
        for k in FAR_FIRST:
            exchange(g, k).start()
        forward(g, 0).start()
        keep(g).start()

    sign = jnp.where(low[:1], 1.0, -1.0).astype(F32)
    piece = lax.broadcasted_iota(jnp.int32, (CH, LANES), 1) // 32

    def block(ref, g, which, ff):
        return jnp.concatenate([ref[g, which * 4 + q, ff] for q in range(4)], axis=1)

    def crossed(ref, g, which, ff):
        parts = [pltpu.roll(ref[g, which * 4 + q, ff].astype(F32), 64, 1) * sign for q in range(4)]
        return jnp.concatenate(parts, axis=1).astype(BF16)

    def cross(g):
        lower, upper = (own, other) if DIRECTION[g] == DOWN else (other, own)
        for b in range(2):
            left, rest = [], []
            for ff in range(2):
                plain, turned = block(lower, g, b, ff), crossed(lower, g, b, ff)
                tail = [plain[64:], turned[64:]]
                weights = jnp.concatenate([plain[:64], turned[:64]] + tail * 4, axis=0)
                first = block(lower, g, 1, ff) if b == 0 else block(upper, g, 0, ff)
                second = block(upper, g, b, ff)
                streamed = jnp.concatenate([first, second], axis=0)
                product = lax.dot_general(streamed, weights, (((1,), (1,)), ((), ())),
                                          preferred_element_type=F32)
                for r in range(2):
                    part = product[r * CH:(r + 1) * CH]
                    for t in range(4):
                        made[g, b * 4 + t, pl.ds(ff * 32 + r * 16, 16), :] = (
                            part[t * 16:(t + 1) * 16, :LANES].astype(BF16))
                    left.append(part[64:, :LANES])
                    rest.append(part[:, LANES:])
            edge = jnp.where(piece < 2, jnp.where(piece < 1, rest[0], rest[1]),
                             jnp.where(piece < 3, rest[2], rest[3])).astype(BF16)
            for t in range(4):
                fours = jnp.concatenate([a[t * 4:(t + 1) * 4] for a in left], axis=0)
                made[g, b * 4 + t, pl.ds(64, 16), :] = fours.astype(BF16)
                made[g, b * 4 + t, pl.ds(80, 16), :] = edge[t * 16:(t + 1) * 16]
                made[g, b * 4 + t, pl.ds(96, 16), :] = edge[64:]

    def deliver(g, k):
        owner = flip(slot, k)
        step = 0 if DIRECTION[g] == DOWN else -1
        return pltpu.make_async_remote_copy(
            src_ref=made.at[g, owner], dst_ref=got.at[g, slot],
            send_sem=send_r.at[g, k], recv_sem=recv_r.at[g, k],
            device_id=device(plane + step, owner), device_id_type=MESH)

    def retain(g):
        return pltpu.make_async_copy(made.at[g, slot], got.at[g, slot], local.at[GROUPS + g])

    def pass_on(g):
        for k in NEAR_FIRST:
            exchange(g, k).wait_recv()
            forward(g, k).start()

    def work(g):
        keep(g).wait()
        for k in range(SLOTS):
            forward(g, k).wait_recv()
        cross(g)
        if DIRECTION[g] == DOWN:
            retain(g).start()
        for k in FAR_FIRST + ((0,) if DIRECTION[g] == UP else ()):
            deliver(g, k).start()

    pass_on(0)
    pass_on(1)
    pass_on(2)
    work(0)
    pass_on(3)
    work(1)
    work(2)
    work(3)

    for g in range(GROUPS):
        if DIRECTION[g] == DOWN:
            retain(g).wait()
        for k in range(0 if DIRECTION[g] == UP else 1, SLOTS):
            deliver(g, k).wait_recv()

        def spread(d, carry, g=g):
            row = pl.multiple_of((g * SLOTS + d) * ROWS, 16)
            gotf[pl.ds(row, ROWS), :] = got[g, d].astype(F32)
            return carry

        lax.fori_loop(0, SLOTS, spread, 0)

    fetch_lag.wait()
    sources = GROUPS * SLOTS
    low16 = lax.broadcasted_iota(jnp.int32, (16, LANES), 1) // 32

    def rows_of(row):
        return gotf[pl.ds(row, sources, stride=ROWS), :]

    def lags(first, row_main, row_edge, stride_ff, stride_r):
        z = jnp.concatenate([rows_of(row_edge + j) for j in range(4)], axis=0).T
        pieces = []
        for j in range(4):
            for r in range(2):
                total = None
                for ff in range(2):
                    for c in range(2):
                        at = (ff * 4 + r * 2 + c) * 16
                        to = ff * 2 + c
                        moved = z[at:at + 16]
                        if (to - j) % 4:
                            moved = pltpu.roll(moved, ((to - j) % 4) * 32, 1)
                        total = moved if total is None else jnp.where(low16 == to, moved, total)
                pieces.append(total)
        edge = jnp.dot(jnp.concatenate(pieces, axis=0).astype(BF16), lag_ref[1], preferred_element_type=F32)
        for r in range(2):
            for half in range(2):
                rows = []
                for j in (2 * half, 2 * half + 1):
                    for ff in range(2):
                        rows.append(rows_of(row_main + ff * stride_ff + r * stride_r + j))
                z = jnp.concatenate(rows, axis=0).T
                top, bottom = z[:64], z[64:]
                lhs = jnp.concatenate([jnp.where(low, top, pltpu.roll(bottom, 64, 1)),
                                       jnp.where(low, pltpu.roll(top, 64, 1), bottom)], axis=0)
                body = jnp.dot(lhs.astype(BF16), lag_ref[0], preferred_element_type=F32)
                for n in range(2):
                    j = 2 * half + n
                    at = (j * 2 + r) * 16
                    pieces = []
                    for t in range(4):
                        pieces.append(body[n * 64 + t * 16:n * 64 + (t + 1) * 16])
                        pieces.append(edge[at + t * 4:at + (t + 1) * 4])
                    out_ref[r, first + j] = jnp.concatenate(pieces, axis=0).astype(BF16)

    def lags_first(n, carry):
        lags(4 * n, 4 * n, 80 + 4 * n, 32, 16)
        return carry

    lax.fori_loop(0, 4, lags_first, 0)
    lags(16, 64, 96 + 4 * quarter, 8, 4)

    for g in range(GROUPS):
        for k in range(1, SLOTS):
            exchange(g, k).wait_send()
        for k in range(SLOTS):
            forward(g, k).wait_send()
        for k in range(0 if DIRECTION[g] == UP else 1, SLOTS):
            deliver(g, k).wait_send()


def shards(spectra, live_mask):
    windows = spectra.shape[0] * lax.axis_size("tm")
    tables = jnp.asarray(lag_tables(windows))
    vmem = pl.BlockSpec(memory_space=pltpu.VMEM)
    dma = pltpu.SemaphoreType.DMA
    return pl.pallas_call(
        kernel,
        out_shape=jax.ShapeDtypeStruct((2, 20, CH, LANES), BF16),
        in_specs=[pl.BlockSpec(memory_space=pltpu.HBM)] * 3,
        out_specs=vmem,
        scratch_shapes=[
            pltpu.VMEM((WIN, CH, LANES), BF16),
            pltpu.SMEM((CH,), jnp.int32),
            pltpu.VMEM((2, LANES, LANES), BF16),
            pltpu.VMEM((WIN * CH, LANES), F32),
            pltpu.VMEM((64 * CH, LANES), F32),
            pltpu.VMEM((SLOTS, GROUPS, 2, CH, LANES), BF16),
            pltpu.VMEM((GROUPS, SLOTS, 2, CH, LANES), BF16),
            pltpu.VMEM((GROUPS, SLOTS, 2, CH, LANES), BF16),
            pltpu.VMEM((GROUPS, SLOTS, ROWS, LANES), BF16),
            pltpu.VMEM((GROUPS, SLOTS, ROWS, LANES), BF16),
            pltpu.VMEM((GROUPS * SLOTS * ROWS, LANES), F32),
            dma((GROUPS, SLOTS)), dma((GROUPS, SLOTS)),
            dma((GROUPS, SLOTS)), dma((GROUPS, SLOTS)),
            dma((GROUPS, SLOTS)), dma((GROUPS, SLOTS)),
            dma((2 * GROUPS,)), dma((CH // CHUNK + 2,)),
        ],
        compiler_params=pltpu.CompilerParams(
            collective_id=0, has_side_effects=True, vmem_limit_bytes=62 * 2**20),
        name="correlate",
    )(spectra, live_mask, tables)


def solution(mesh):
    placed = (P("tm", "chan", None), P("chan"))
    return jax.shard_map(
        shards, mesh=mesh, in_specs=placed, out_specs=P(None, "tm", "chan", None), check_vma=False
    )
```

```python
import functools
import math

import jax
import jax.numpy as jnp
import ml_dtypes
import numpy as np
from jax import lax
from jax.experimental import pallas as pl
from jax.experimental.pallas import tpu as pltpu
from jax.sharding import PartitionSpec as P

MESH = pl.DeviceIdType.MESH
F32, BF16 = jnp.float32, jnp.bfloat16
PLANES = 64
SLOTS = 8
CH = 80
WIN = 64
LANES = 128
GROUPS = 4
ROWS = 112
DOWN, UP = 0, 1
DIRECTION = (DOWN, DOWN, DOWN, DOWN)
CHUNK = 16
NEAR_FIRST = (2, 3, 6, 7, 4, 5)
SEND_ORDER = (1, 4, 5, 6, 7, 2, 3)


def lag_tables(windows_all):
    bins = np.arange(64)
    shifts = np.arange(128) - 64
    phase = 2.0 * np.pi / 128 * bins[:, None] * shifts[None, :]
    weight = np.where(bins == 0, 1.0, 2.0)
    scaling = 1.0 / (2.0 * math.sqrt(64 * windows_all))
    parts = np.stack([weight[:, None] * np.cos(phase), -weight[:, None] * np.sin(phase)]) * scaling
    parts = parts.reshape(2, SLOTS, GROUPS, 2, LANES)
    main = parts.transpose(0, 3, 2, 1, 4).reshape(LANES, LANES)
    rest = parts.transpose(3, 0, 2, 1, 4).reshape(LANES, LANES)
    return np.stack([main, rest]).astype(ml_dtypes.bfloat16)


def flip(slot, bits):
    for bit in range(3):
        if bits >> bit & 1:
            step = 1 << bit
            slot = slot + step - 2 * step * ((slot // step) % 2)
    return slot


def device(plane, slot):
    plane = (plane + PLANES) % PLANES
    return (plane * 2 + slot // 4, slot % 4)


def kernel(x_hbm, mask_hbm, lag_hbm, out_ref, x_ref, mask_ref, lag_ref, xf, tf, sent, own, other, made, got, gotf,
           send_a, recv_a, send_z, recv_z, send_r, recv_r, local, load):
    plane = lax.axis_index("chan") // 2
    quarter = lax.axis_index("tm")
    slot = (lax.axis_index("chan") % 2) * 4 + quarter
    any_up = UP in DIRECTION

    def fetch(n):
        part = (slice(None), pl.ds(pl.multiple_of(n * CHUNK, CHUNK), CHUNK), slice(None))
        return pltpu.make_async_copy(x_hbm.at[part], x_ref.at[part], load.at[n])

    chunks = CH // CHUNK
    fetch_mask = pltpu.make_async_copy(mask_hbm, mask_ref, load.at[chunks])
    fetch_lag = pltpu.make_async_copy(lag_hbm, lag_ref, load.at[chunks + 1])
    fetch_mask.start()
    for n in range(chunks):
        fetch(n).start()
    fetch_lag.start()

    barrier = pltpu.get_barrier_semaphore()
    greeted = [device(plane, flip(slot, k)) for k in range(1, SLOTS)]
    for step in (-1, 1):
        greeted += [device(plane + step, flip(slot, k)) for k in range(SLOTS if any_up else 1)]
    for target in greeted:
        pl.semaphore_signal(barrier, inc=1, device_id=target, device_id_type=MESH)

    lane = lax.broadcasted_iota(jnp.int32, (64, LANES), 1)
    low = lane < 64

    def turn(channel):
        t, m = channel // 20, channel % 20
        place = 16 * t + m + (m // 16) * (48 - 12 * t)
        pair = [xf[pl.ds(channel + k, WIN, stride=CH), :] for k in range(2)]
        z = jnp.concatenate(pair, axis=0).astype(BF16).T.astype(F32)
        power = jnp.sum(z * z, axis=0, keepdims=True) * (1.0 / LANES)
        live0 = mask_ref[channel].astype(F32)
        live1 = mask_ref[channel + 1].astype(F32)
        z = z * (lax.rsqrt(power + 1e-6) * jnp.where(low[:1], live0, live1))
        top, bottom = z[:64], z[64:]
        tf[pl.ds(place, 64, stride=CH), :] = jnp.where(low, top, pltpu.roll(bottom, 64, 1))
        tf[pl.ds(place + 1, 64, stride=CH), :] = jnp.where(low, pltpu.roll(top, 64, 1), bottom)

    def prepare(n, carry):
        fetch(n).wait()
        first = pl.multiple_of(n * CHUNK, CHUNK)

        def widen(w, c):
            for k in range(8):
                row = pl.multiple_of((w * 8 + k) * CH + first, CHUNK)
                xf[pl.ds(row, CHUNK), :] = x_ref[w * 8 + k, pl.ds(first, CHUNK), :].astype(F32)
            return c

        lax.fori_loop(0, WIN // 8, widen, 0)
        for k in range(0, CHUNK, 2):
            turn(first + k)
        return carry

    fetch_mask.wait()
    lax.fori_loop(0, chunks, prepare, 0)

    def exchange(g, k):
        peer = flip(slot, k)
        return pltpu.make_async_remote_copy(
            src_ref=sent.at[peer, g], dst_ref=own.at[g, slot],
            send_sem=send_a.at[g, k], recv_sem=recv_a.at[g, k],
            device_id=device(plane, peer), device_id_type=MESH)

    def keep(g):
        return pltpu.make_async_copy(sent.at[slot, g], own.at[g, slot], local.at[g])

    def forward(g, k):
        step = -1 if DIRECTION[g] == DOWN else 1
        source = flip(slot, k)
        return pltpu.make_async_remote_copy(
            src_ref=own.at[g, source] if k else sent.at[slot, g], dst_ref=other.at[g, source],
            send_sem=send_z.at[g, k], recv_sem=recv_z.at[g, k],
            device_id=device(plane + step, slot), device_id_type=MESH)

    for g in range(GROUPS):
        def narrow(d, carry, g=g):
            for ff in range(2):
                row = pl.multiple_of((d * 8 + g * 2 + ff) * CH, 16)
                sent[d, g, ff] = tf[pl.ds(row, CH), :].astype(BF16)
            return carry

        lax.fori_loop(0, SLOTS, narrow, 0)
        if g == 0:
            pl.semaphore_wait(barrier, len(greeted))
        for k in SEND_ORDER:
            exchange(g, k).start()
        forward(g, 0).start()
        keep(g).start()

    sign = jnp.where(low[:1], 1.0, -1.0).astype(F32)
    piece = lax.broadcasted_iota(jnp.int32, (CH, LANES), 1) // 32

    def block(ref, g, which, ff):
        return jnp.concatenate([ref[g, which * 4 + q, ff] for q in range(4)], axis=1)

    def crossed(ref, g, which, ff):
        parts = [pltpu.roll(ref[g, which * 4 + q, ff].astype(F32), 64, 1) * sign for q in range(4)]
        return jnp.concatenate(parts, axis=1).astype(BF16)

    def cross(g):
        lower, upper = (own, other) if DIRECTION[g] == DOWN else (other, own)
        for b in range(2):
            left, rest = [], []
            for ff in range(2):
                plain, turned = block(lower, g, b, ff), crossed(lower, g, b, ff)
                tail = [plain[64:], turned[64:]]
                weights = jnp.concatenate([plain[:64], turned[:64]] + tail * 4, axis=0)
                first = block(lower, g, 1, ff) if b == 0 else block(upper, g, 0, ff)
                second = block(upper, g, b, ff)
                streamed = jnp.concatenate([first, second], axis=0)
                product = lax.dot_general(streamed, weights, (((1,), (1,)), ((), ())),
                                          preferred_element_type=F32)
                for r in range(2):
                    part = product[r * CH:(r + 1) * CH]
                    for t in range(4):
                        made[g, b * 4 + t, pl.ds(ff * 32 + r * 16, 16), :] = (
                            part[t * 16:(t + 1) * 16, :LANES].astype(BF16))
                    left.append(part[64:, :LANES])
                    rest.append(part[:, LANES:])
            edge = jnp.where(piece < 2, jnp.where(piece < 1, rest[0], rest[1]),
                             jnp.where(piece < 3, rest[2], rest[3])).astype(BF16)
            for t in range(4):
                fours = jnp.concatenate([a[t * 4:(t + 1) * 4] for a in left], axis=0)
                made[g, b * 4 + t, pl.ds(64, 16), :] = fours.astype(BF16)
                made[g, b * 4 + t, pl.ds(80, 16), :] = edge[t * 16:(t + 1) * 16]
                made[g, b * 4 + t, pl.ds(96, 16), :] = edge[64:]

    def deliver(g, k):
        owner = flip(slot, k)
        step = 0 if DIRECTION[g] == DOWN else -1
        return pltpu.make_async_remote_copy(
            src_ref=made.at[g, owner], dst_ref=got.at[g, slot],
            send_sem=send_r.at[g, k], recv_sem=recv_r.at[g, k],
            device_id=device(plane + step, owner), device_id_type=MESH)

    def retain(g):
        return pltpu.make_async_copy(made.at[g, slot], got.at[g, slot], local.at[GROUPS + g])

    def pass_on(g):
        for k in NEAR_FIRST:
            exchange(g, k).wait_recv()
            forward(g, k).start()

    def work(g):
        keep(g).wait()
        for k in range(SLOTS):
            forward(g, k).wait_recv()
        cross(g)
        if DIRECTION[g] == DOWN:
            retain(g).start()
        for k in SEND_ORDER + ((0,) if DIRECTION[g] == UP else ()):
            deliver(g, k).start()

    for g in range(GROUPS):
        exchange(g, 1).wait_recv()
        forward(g, 1).start()
    pass_on(0)
    pass_on(1)
    pass_on(2)
    work(0)
    pass_on(3)
    work(1)
    work(2)
    work(3)

    for g in range(GROUPS):
        if DIRECTION[g] == DOWN:
            retain(g).wait()
        for k in range(0 if DIRECTION[g] == UP else 1, SLOTS):
            deliver(g, k).wait_recv()

        def spread(d, carry, g=g):
            row = pl.multiple_of((g * SLOTS + d) * ROWS, 16)
            gotf[pl.ds(row, ROWS), :] = got[g, d].astype(F32)
            return carry

        lax.fori_loop(0, SLOTS, spread, 0)

    fetch_lag.wait()
    sources = GROUPS * SLOTS
    low16 = lax.broadcasted_iota(jnp.int32, (16, LANES), 1) // 32

    def rows_of(row):
        return gotf[pl.ds(row, sources, stride=ROWS), :]

    def lags(first, row_main, row_edge, stride_ff, stride_r):
        z = jnp.concatenate([rows_of(row_edge + j) for j in range(4)], axis=0).T
        pieces = []
        for j in range(4):
            for r in range(2):
                total = None
                for ff in range(2):
                    for c in range(2):
                        at = (ff * 4 + r * 2 + c) * 16
                        to = ff * 2 + c
                        moved = z[at:at + 16]
                        if (to - j) % 4:
                            moved = pltpu.roll(moved, ((to - j) % 4) * 32, 1)
                        total = moved if total is None else jnp.where(low16 == to, moved, total)
                pieces.append(total)
        edge = jnp.dot(jnp.concatenate(pieces, axis=0).astype(BF16), lag_ref[1], preferred_element_type=F32)
        for r in range(2):
            for half in range(2):
                rows = []
                for j in (2 * half, 2 * half + 1):
                    for ff in range(2):
                        rows.append(rows_of(row_main + ff * stride_ff + r * stride_r + j))
                z = jnp.concatenate(rows, axis=0).T
                top, bottom = z[:64], z[64:]
                lhs = jnp.concatenate([jnp.where(low, top, pltpu.roll(bottom, 64, 1)),
                                       jnp.where(low, pltpu.roll(top, 64, 1), bottom)], axis=0)
                body = jnp.dot(lhs.astype(BF16), lag_ref[0], preferred_element_type=F32)
                for n in range(2):
                    j = 2 * half + n
                    at = (j * 2 + r) * 16
                    pieces = []
                    for t in range(4):
                        pieces.append(body[n * 64 + t * 16:n * 64 + (t + 1) * 16])
                        pieces.append(edge[at + t * 4:at + (t + 1) * 4])
                    out_ref[r, first + j] = jnp.concatenate(pieces, axis=0).astype(BF16)

    def lags_first(n, carry):
        lags(4 * n, 4 * n, 80 + 4 * n, 32, 16)
        return carry

    lax.fori_loop(0, 4, lags_first, 0)
    lags(16, 64, 96 + 4 * quarter, 8, 4)

    for g in range(GROUPS):
        for k in range(1, SLOTS):
            exchange(g, k).wait_send()
        for k in range(SLOTS):
            forward(g, k).wait_send()
        for k in range(0 if DIRECTION[g] == UP else 1, SLOTS):
            deliver(g, k).wait_send()


def shards(spectra, live_mask):
    windows = spectra.shape[0] * lax.axis_size("tm")
    tables = jnp.asarray(lag_tables(windows))
    vmem = pl.BlockSpec(memory_space=pltpu.VMEM)
    dma = pltpu.SemaphoreType.DMA
    return pl.pallas_call(
        kernel,
        out_shape=jax.ShapeDtypeStruct((2, 20, CH, LANES), BF16),
        in_specs=[pl.BlockSpec(memory_space=pltpu.HBM)] * 3,
        out_specs=vmem,
        scratch_shapes=[
            pltpu.VMEM((WIN, CH, LANES), BF16),
            pltpu.SMEM((CH,), jnp.int32),
            pltpu.VMEM((2, LANES, LANES), BF16),
            pltpu.VMEM((WIN * CH, LANES), F32),
            pltpu.VMEM((64 * CH, LANES), F32),
            pltpu.VMEM((SLOTS, GROUPS, 2, CH, LANES), BF16),
            pltpu.VMEM((GROUPS, SLOTS, 2, CH, LANES), BF16),
            pltpu.VMEM((GROUPS, SLOTS, 2, CH, LANES), BF16),
            pltpu.VMEM((GROUPS, SLOTS, ROWS, LANES), BF16),
            pltpu.VMEM((GROUPS, SLOTS, ROWS, LANES), BF16),
            pltpu.VMEM((GROUPS * SLOTS * ROWS, LANES), F32),
            dma((GROUPS, SLOTS)), dma((GROUPS, SLOTS)),
            dma((GROUPS, SLOTS)), dma((GROUPS, SLOTS)),
            dma((GROUPS, SLOTS)), dma((GROUPS, SLOTS)),
            dma((2 * GROUPS,)), dma((CH // CHUNK + 2,)),
        ],
        compiler_params=pltpu.CompilerParams(
            collective_id=0, has_side_effects=True, vmem_limit_bytes=40 * 2**20),
        name="correlate",
    )(*(pltpu.with_memory_space_constraint(a, pltpu.HBM) for a in (spectra, live_mask, tables)))


def solution(mesh):
    placed = (P("tm", "chan", None), P("chan"))
    return jax.shard_map(
        shards, mesh=mesh, in_specs=placed, out_specs=P(None, "tm", "chan", None), check_vma=False
    )
```

```python
import functools
import math

import jax
import jax.numpy as jnp
import ml_dtypes
import numpy as np
from jax import lax
from jax.experimental import pallas as pl
from jax.experimental.pallas import tpu as pltpu
from jax.sharding import PartitionSpec as P

MESH = pl.DeviceIdType.MESH
F32, BF16 = jnp.float32, jnp.bfloat16
PLANES = 64
SLOTS = 8
CH = 80
WIN = 64
LANES = 128
GROUPS = 4
ROWS = 112
DOWN, UP = 0, 1
DIRECTION = (DOWN, DOWN, DOWN, DOWN)
CHUNK = 16
NEAR_FIRST = (2, 3, 6, 7, 4, 5)
SEND_ORDER = (1, 4, 5, 6, 7, 2, 3)


def lag_tables(windows_all):
    bins = np.arange(64)
    shifts = np.arange(128) - 64
    phase = 2.0 * np.pi / 128 * bins[:, None] * shifts[None, :]
    weight = np.where(bins == 0, 1.0, 2.0)
    scaling = 1.0 / (2.0 * math.sqrt(64 * windows_all))
    parts = np.stack([weight[:, None] * np.cos(phase), -weight[:, None] * np.sin(phase)]) * scaling
    parts = parts.reshape(2, SLOTS, GROUPS, 2, LANES)
    tables = []
    for half in range(2):
        here = parts[:, :, 2 * half:2 * half + 2]
        main = here.transpose(0, 3, 2, 1, 4).reshape(2, 1, 32, LANES)
        rest = here.transpose(3, 0, 2, 1, 4).reshape(4, 1, 16, LANES)
        main = np.broadcast_to(main, (2, 4, 32, LANES)).reshape(256, LANES)
        rest = np.broadcast_to(rest, (4, 8, 16, LANES)).reshape(512, LANES)
        tables.append(np.concatenate([main, rest]))
    return np.stack(tables).astype(ml_dtypes.bfloat16)


def flip(slot, bits):
    for bit in range(3):
        if bits >> bit & 1:
            step = 1 << bit
            slot = slot + step - 2 * step * ((slot // step) % 2)
    return slot


def device(plane, slot):
    plane = (plane + PLANES) % PLANES
    return (plane * 2 + slot // 4, slot % 4)


def kernel(x_hbm, mask_hbm, lag_hbm, out_ref, x_ref, mask_ref, lag_ref, xf, tf, sent, own, other, made, got, gotf, acc,
           send_a, recv_a, send_z, recv_z, send_r, recv_r, local, load):
    plane = lax.axis_index("chan") // 2
    quarter = lax.axis_index("tm")
    slot = (lax.axis_index("chan") % 2) * 4 + quarter
    any_up = UP in DIRECTION

    def fetch(n):
        part = (slice(None), pl.ds(pl.multiple_of(n * CHUNK, CHUNK), CHUNK), slice(None))
        return pltpu.make_async_copy(x_hbm.at[part], x_ref.at[part], load.at[n])

    chunks = CH // CHUNK
    fetch_mask = pltpu.make_async_copy(mask_hbm, mask_ref, load.at[chunks])
    fetch_lag = pltpu.make_async_copy(lag_hbm, lag_ref, load.at[chunks + 1])
    fetch_mask.start()
    for n in range(chunks):
        fetch(n).start()
    fetch_lag.start()

    barrier = pltpu.get_barrier_semaphore()
    greeted = [device(plane, flip(slot, k)) for k in range(1, SLOTS)]
    for step in (-1, 1):
        greeted += [device(plane + step, flip(slot, k)) for k in range(SLOTS if any_up else 1)]
    for target in greeted:
        pl.semaphore_signal(barrier, inc=1, device_id=target, device_id_type=MESH)

    lane = lax.broadcasted_iota(jnp.int32, (64, LANES), 1)
    low = lane < 64

    def turn(channel):
        t, m = channel // 20, channel % 20
        place = 16 * t + m + (m // 16) * (48 - 12 * t)
        pair = [xf[pl.ds(channel + k, WIN, stride=CH), :] for k in range(2)]
        z = jnp.concatenate(pair, axis=0).astype(BF16).T.astype(F32)
        power = jnp.sum(z * z, axis=0, keepdims=True) * (1.0 / LANES)
        live0 = mask_ref[channel].astype(F32)
        live1 = mask_ref[channel + 1].astype(F32)
        z = z * (lax.rsqrt(power + 1e-6) * jnp.where(low[:1], live0, live1))
        top, bottom = z[:64], z[64:]
        tf[pl.ds(place, 64, stride=CH), :] = jnp.where(low, top, pltpu.roll(bottom, 64, 1))
        tf[pl.ds(place + 1, 64, stride=CH), :] = jnp.where(low, pltpu.roll(top, 64, 1), bottom)

    def prepare(n, carry):
        fetch(n).wait()
        first = pl.multiple_of(n * CHUNK, CHUNK)

        def widen(w, c):
            for k in range(8):
                row = pl.multiple_of((w * 8 + k) * CH + first, CHUNK)
                xf[pl.ds(row, CHUNK), :] = x_ref[w * 8 + k, pl.ds(first, CHUNK), :].astype(F32)
            return c

        lax.fori_loop(0, WIN // 8, widen, 0)
        for k in range(0, CHUNK, 2):
            turn(first + k)
        return carry

    fetch_mask.wait()
    lax.fori_loop(0, chunks, prepare, 0)

    def exchange(g, k):
        peer = flip(slot, k)
        return pltpu.make_async_remote_copy(
            src_ref=sent.at[peer, g], dst_ref=own.at[g, slot],
            send_sem=send_a.at[g, k], recv_sem=recv_a.at[g, k],
            device_id=device(plane, peer), device_id_type=MESH)

    def keep(g):
        return pltpu.make_async_copy(sent.at[slot, g], own.at[g, slot], local.at[g])

    def forward(g, k):
        step = -1 if DIRECTION[g] == DOWN else 1
        source = flip(slot, k)
        return pltpu.make_async_remote_copy(
            src_ref=own.at[g, source] if k else sent.at[slot, g], dst_ref=other.at[g, source],
            send_sem=send_z.at[g, k], recv_sem=recv_z.at[g, k],
            device_id=device(plane + step, slot), device_id_type=MESH)

    for g in range(GROUPS):
        def narrow(d, carry, g=g):
            for ff in range(2):
                row = pl.multiple_of((d * 8 + g * 2 + ff) * CH, 16)
                sent[d, g, ff] = tf[pl.ds(row, CH), :].astype(BF16)
            return carry

        lax.fori_loop(0, SLOTS, narrow, 0)
        if g == 0:
            pl.semaphore_wait(barrier, len(greeted))
        for k in SEND_ORDER:
            exchange(g, k).start()
        forward(g, 0).start()
        keep(g).start()

    sign = jnp.where(low[:1], 1.0, -1.0).astype(F32)
    piece = lax.broadcasted_iota(jnp.int32, (CH, LANES), 1) // 32

    def block(ref, g, which, ff):
        return jnp.concatenate([ref[g, which * 4 + q, ff] for q in range(4)], axis=1)

    def crossed(ref, g, which, ff):
        parts = [pltpu.roll(ref[g, which * 4 + q, ff].astype(F32), 64, 1) * sign for q in range(4)]
        return jnp.concatenate(parts, axis=1).astype(BF16)

    def cross(g):
        lower, upper = (own, other) if DIRECTION[g] == DOWN else (other, own)
        for b in range(2):
            left, rest = [], []
            for ff in range(2):
                plain, turned = block(lower, g, b, ff), crossed(lower, g, b, ff)
                tail = [plain[64:], turned[64:]]
                weights = jnp.concatenate([plain[:64], turned[:64]] + tail * 4, axis=0)
                first = block(lower, g, 1, ff) if b == 0 else block(upper, g, 0, ff)
                second = block(upper, g, b, ff)
                streamed = jnp.concatenate([first, second], axis=0)
                product = lax.dot_general(streamed, weights, (((1,), (1,)), ((), ())),
                                          preferred_element_type=F32)
                for r in range(2):
                    part = product[r * CH:(r + 1) * CH]
                    for t in range(4):
                        made[g, b * 4 + t, pl.ds(ff * 32 + r * 16, 16), :] = (
                            part[t * 16:(t + 1) * 16, :LANES].astype(BF16))
                    left.append(part[64:, :LANES])
                    rest.append(part[:, LANES:])
            edge = jnp.where(piece < 2, jnp.where(piece < 1, rest[0], rest[1]),
                             jnp.where(piece < 3, rest[2], rest[3])).astype(BF16)
            for t in range(4):
                fours = jnp.concatenate([a[t * 4:(t + 1) * 4] for a in left], axis=0)
                made[g, b * 4 + t, pl.ds(64, 16), :] = fours.astype(BF16)
                made[g, b * 4 + t, pl.ds(80, 16), :] = edge[t * 16:(t + 1) * 16]
                made[g, b * 4 + t, pl.ds(96, 16), :] = edge[64:]

    def deliver(g, k):
        owner = flip(slot, k)
        step = 0 if DIRECTION[g] == DOWN else -1
        return pltpu.make_async_remote_copy(
            src_ref=made.at[g, owner], dst_ref=got.at[g, slot],
            send_sem=send_r.at[g, k], recv_sem=recv_r.at[g, k],
            device_id=device(plane + step, owner), device_id_type=MESH)

    def retain(g):
        return pltpu.make_async_copy(made.at[g, slot], got.at[g, slot], local.at[GROUPS + g])

    def pass_on(g):
        for k in NEAR_FIRST:
            exchange(g, k).wait_recv()
            forward(g, k).start()

    def work(g):
        keep(g).wait()
        for k in range(SLOTS):
            forward(g, k).wait_recv()
        cross(g)
        if DIRECTION[g] == DOWN:
            retain(g).start()
        for k in SEND_ORDER + ((0,) if DIRECTION[g] == UP else ()):
            deliver(g, k).start()

    for g in range(GROUPS):
        exchange(g, 1).wait_recv()
        forward(g, 1).start()
    pass_on(0)
    pass_on(1)
    lane128 = lax.broadcasted_iota(jnp.int32, (64, LANES), 1)

    def collect(g):
        retain(g).wait()
        for k in range(1, SLOTS):
            deliver(g, k).wait_recv()

        def spread(d, carry):
            row = pl.multiple_of((g * SLOTS + d) * ROWS, 16)
            gotf[pl.ds(row, ROWS), :] = got[g, d].astype(F32)
            return carry

        lax.fori_loop(0, SLOTS, spread, 0)

    def lags(half, first, row_main, row_edge, stride_ff, stride_r):
        def rows_of(row):
            return gotf[pl.ds(half * 16 * ROWS + row, 16, stride=ROWS), :]

        z = jnp.concatenate([rows_of(row_edge + j) for j in range(4)] + [jnp.zeros((64, LANES), F32)], axis=0).T
        pieces = []
        for j in range(4):
            mine = lane128[:16] // 16 == j
            for r in range(2):
                blocks = [z[(ff * 4 + r * 2 + c) * 16:][:16] for ff in range(2) for c in range(2)]
                pieces.append(jnp.concatenate([jnp.where(mine, p, 0.0) for p in blocks], axis=1))
        edge = jnp.dot(jnp.concatenate(pieces, axis=0).astype(BF16), lag_ref[half, pl.ds(256, 512), :],
                       preferred_element_type=F32)
        for r in range(2):
            rows = [rows_of(row_main + ff * stride_ff + r * stride_r + j) for j in range(4) for ff in range(2)]
            z = jnp.concatenate(rows, axis=0).T
            lhs = []
            for j in range(4):
                mine = lane128 // 32 == j
                lhs.append(jnp.concatenate([jnp.where(mine, z[:64], 0.0), jnp.where(mine, z[64:], 0.0)], axis=1))
            body = jnp.dot(jnp.concatenate(lhs, axis=0).astype(BF16), lag_ref[half, pl.ds(0, 256), :],
                           preferred_element_type=F32)
            for j in range(4):
                at = (j * 2 + r) * 16
                pieces = []
                for t in range(4):
                    pieces.append(body[j * 64 + t * 16:j * 64 + (t + 1) * 16])
                    pieces.append(edge[at + t * 4:at + (t + 1) * 4])
                value = jnp.concatenate(pieces, axis=0)
                if half == 0:
                    acc[r, first + j] = value
                else:
                    out_ref[r, first + j] = (acc[r, first + j] + value).astype(BF16)

    def transform(half):
        def lags_first(n, carry):
            lags(half, 4 * n, 4 * n, 80 + 4 * n, 32, 16)
            return carry

        lax.fori_loop(0, 4, lags_first, 0)
        lags(half, 16, 64, 96 + 4 * quarter, 8, 4)

    pass_on(2)
    work(0)
    pass_on(3)
    work(1)
    work(2)
    fetch_lag.wait()
    collect(0)
    collect(1)
    transform(0)
    collect(2)
    work(3)
    collect(3)
    transform(1)

    for g in range(GROUPS):
        for k in range(1, SLOTS):
            exchange(g, k).wait_send()
        for k in range(SLOTS):
            forward(g, k).wait_send()
        for k in range(0 if DIRECTION[g] == UP else 1, SLOTS):
            deliver(g, k).wait_send()


def shards(spectra, live_mask):
    windows = spectra.shape[0] * lax.axis_size("tm")
    tables = jnp.asarray(lag_tables(windows))
    vmem = pl.BlockSpec(memory_space=pltpu.VMEM)
    dma = pltpu.SemaphoreType.DMA
    return pl.pallas_call(
        kernel,
        out_shape=jax.ShapeDtypeStruct((2, 20, CH, LANES), BF16),
        in_specs=[pl.BlockSpec(memory_space=pltpu.HBM)] * 3,
        out_specs=vmem,
        scratch_shapes=[
            pltpu.VMEM((WIN, CH, LANES), BF16),
            pltpu.SMEM((CH,), jnp.int32),
            pltpu.VMEM((2, 768, LANES), BF16),
            pltpu.VMEM((WIN * CH, LANES), F32),
            pltpu.VMEM((64 * CH, LANES), F32),
            pltpu.VMEM((SLOTS, GROUPS, 2, CH, LANES), BF16),
            pltpu.VMEM((GROUPS, SLOTS, 2, CH, LANES), BF16),
            pltpu.VMEM((GROUPS, SLOTS, 2, CH, LANES), BF16),
            pltpu.VMEM((GROUPS, SLOTS, ROWS, LANES), BF16),
            pltpu.VMEM((GROUPS, SLOTS, ROWS, LANES), BF16),
            pltpu.VMEM((GROUPS * SLOTS * ROWS, LANES), F32),
            pltpu.VMEM((2, 20, CH, LANES), F32),
            dma((GROUPS, SLOTS)), dma((GROUPS, SLOTS)),
            dma((GROUPS, SLOTS)), dma((GROUPS, SLOTS)),
            dma((GROUPS, SLOTS)), dma((GROUPS, SLOTS)),
            dma((2 * GROUPS,)), dma((CH // CHUNK + 2,)),
        ],
        compiler_params=pltpu.CompilerParams(
            collective_id=0, has_side_effects=True, vmem_limit_bytes=40 * 2**20),
        name="correlate",
    )(*(pltpu.with_memory_space_constraint(a, pltpu.HBM) for a in (spectra, live_mask, tables)))


def solution(mesh):
    placed = (P("tm", "chan", None), P("chan"))
    return jax.shard_map(
        shards, mesh=mesh, in_specs=placed, out_specs=P(None, "tm", "chan", None), check_vma=False
    )
```

```python
import functools
import math

import jax
import jax.numpy as jnp
import ml_dtypes
import numpy as np
from jax import lax
from jax.experimental import pallas as pl
from jax.experimental.pallas import tpu as pltpu
from jax.sharding import PartitionSpec as P

MESH = pl.DeviceIdType.MESH
F32, BF16 = jnp.float32, jnp.bfloat16
PLANES = 64
SLOTS = 8
CH = 80
WIN = 64
LANES = 128
GROUPS = 4
ROWS = 112
DOWN, UP = 0, 1
DIRECTION = (DOWN, DOWN, DOWN, DOWN)
CHUNK = 16
NEAR_FIRST = (2, 3, 6, 7, 4, 5)
SEND_ORDER = (1, 4, 5, 6, 7, 2, 3)


def lag_tables(windows_all):
    bins = np.arange(64)
    shifts = np.arange(128) - 64
    phase = 2.0 * np.pi / 128 * bins[:, None] * shifts[None, :]
    weight = np.where(bins == 0, 1.0, 2.0)
    scaling = 1.0 / (2.0 * math.sqrt(64 * windows_all))
    parts = np.stack([weight[:, None] * np.cos(phase), -weight[:, None] * np.sin(phase)]) * scaling
    parts = parts.reshape(2, SLOTS, GROUPS, 2, LANES)
    main = parts.transpose(0, 3, 2, 1, 4).reshape(LANES, LANES)
    rest = parts.transpose(3, 0, 2, 1, 4).reshape(LANES, LANES)
    return np.stack([main, rest]).astype(ml_dtypes.bfloat16)


def flip(slot, bits):
    for bit in range(3):
        if bits >> bit & 1:
            step = 1 << bit
            slot = slot + step - 2 * step * ((slot // step) % 2)
    return slot


def device(plane, slot):
    plane = (plane + PLANES) % PLANES
    return (plane * 2 + slot // 4, slot % 4)


def kernel(x_hbm, mask_hbm, lag_hbm, out_ref, x_ref, mask_ref, lag_ref, xf, tf, sent, own, other, made, got, gotf,
           send_a, recv_a, send_z, recv_z, send_r, recv_r, local, load):
    plane = lax.axis_index("chan") // 2
    quarter = lax.axis_index("tm")
    slot = (lax.axis_index("chan") % 2) * 4 + quarter
    any_up = UP in DIRECTION

    def fetch(n):
        part = (slice(None), pl.ds(pl.multiple_of(n * CHUNK, CHUNK), CHUNK), slice(None))
        return pltpu.make_async_copy(x_hbm.at[part], x_ref.at[part], load.at[n])

    chunks = CH // CHUNK
    fetch_mask = pltpu.make_async_copy(mask_hbm, mask_ref, load.at[chunks])
    fetch_lag = pltpu.make_async_copy(lag_hbm, lag_ref, load.at[chunks + 1])
    fetch_mask.start()
    for n in range(chunks):
        fetch(n).start()
    fetch_lag.start()

    barrier = pltpu.get_barrier_semaphore()
    greeted = [device(plane, flip(slot, k)) for k in range(1, SLOTS)]
    for step in (-1, 1):
        greeted += [device(plane + step, flip(slot, k)) for k in range(SLOTS if any_up else 1)]
    for target in greeted:
        pl.semaphore_signal(barrier, inc=1, device_id=target, device_id_type=MESH)

    lane = lax.broadcasted_iota(jnp.int32, (64, LANES), 1)
    low = lane < 64

    def turn(channel):
        t, m = channel // 20, channel % 20
        place = 16 * t + m + (m // 16) * (48 - 12 * t)
        pair = [xf[pl.ds(channel + k, WIN, stride=CH), :] for k in range(2)]
        z = jnp.concatenate(pair, axis=0).astype(BF16).T.astype(F32)
        power = jnp.sum(z * z, axis=0, keepdims=True) * (1.0 / LANES)
        live0 = mask_ref[channel].astype(F32)
        live1 = mask_ref[channel + 1].astype(F32)
        z = z * (lax.rsqrt(power + 1e-6) * jnp.where(low[:1], live0, live1))
        top, bottom = z[:64], z[64:]
        tf[pl.ds(place, 64, stride=CH), :] = jnp.where(low, top, pltpu.roll(bottom, 64, 1))
        tf[pl.ds(place + 1, 64, stride=CH), :] = jnp.where(low, pltpu.roll(top, 64, 1), bottom)

    def prepare(n, carry):
        fetch(n).wait()
        first = pl.multiple_of(n * CHUNK, CHUNK)

        def widen(w, c):
            for k in range(8):
                row = pl.multiple_of((w * 8 + k) * CH + first, CHUNK)
                xf[pl.ds(row, CHUNK), :] = x_ref[w * 8 + k, pl.ds(first, CHUNK), :].astype(F32)
            return c

        lax.fori_loop(0, WIN // 8, widen, 0)
        for k in range(0, CHUNK, 2):
            turn(first + k)
        return carry

    fetch_mask.wait()
    lax.fori_loop(0, chunks, prepare, 0)

    def exchange(g, k):
        peer = flip(slot, k)
        return pltpu.make_async_remote_copy(
            src_ref=sent.at[peer, g], dst_ref=own.at[g, slot],
            send_sem=send_a.at[g, k], recv_sem=recv_a.at[g, k],
            device_id=device(plane, peer), device_id_type=MESH)

    def keep(g):
        return pltpu.make_async_copy(sent.at[slot, g], own.at[g, slot], local.at[g])

    def forward(g, k):
        step = -1 if DIRECTION[g] == DOWN else 1
        source = flip(slot, k)
        return pltpu.make_async_remote_copy(
            src_ref=own.at[g, source] if k else sent.at[slot, g], dst_ref=other.at[g, source],
            send_sem=send_z.at[g, k], recv_sem=recv_z.at[g, k],
            device_id=device(plane + step, slot), device_id_type=MESH)

    for g in range(GROUPS):
        def narrow(d, carry, g=g):
            for ff in range(2):
                row = pl.multiple_of((d * 8 + g * 2 + ff) * CH, 16)
                sent[d, g, ff] = tf[pl.ds(row, CH), :].astype(BF16)
            return carry

        lax.fori_loop(0, SLOTS, narrow, 0)
        if g == 0:
            pl.semaphore_wait(barrier, len(greeted))
        for k in SEND_ORDER:
            exchange(g, k).start()
        forward(g, 0).start()
        keep(g).start()

    sign = jnp.where(low[:1], 1.0, -1.0).astype(F32)
    piece = lax.broadcasted_iota(jnp.int32, (CH, LANES), 1) // 32

    def block(ref, g, which, ff):
        return jnp.concatenate([ref[g, which * 4 + q, ff] for q in range(4)], axis=1)

    def crossed(ref, g, which, ff):
        parts = [pltpu.roll(ref[g, which * 4 + q, ff].astype(F32), 64, 1) * sign for q in range(4)]
        return jnp.concatenate(parts, axis=1).astype(BF16)

    def cross(g):
        lower, upper = (own, other) if DIRECTION[g] == DOWN else (other, own)
        for b in range(2):
            left, rest = [], []
            for ff in range(2):
                plain, turned = block(lower, g, b, ff), crossed(lower, g, b, ff)
                tail = [plain[64:], turned[64:]]
                weights = jnp.concatenate([plain[:64], turned[:64]] + tail * 4, axis=0)
                first = block(lower, g, 1, ff) if b == 0 else block(upper, g, 0, ff)
                second = block(upper, g, b, ff)
                streamed = jnp.concatenate([first, second], axis=0)
                product = lax.dot_general(streamed, weights, (((1,), (1,)), ((), ())),
                                          preferred_element_type=F32)
                for r in range(2):
                    part = product[r * CH:(r + 1) * CH]
                    for t in range(4):
                        made[g, b * 4 + t, pl.ds(ff * 32 + r * 16, 16), :] = (
                            part[t * 16:(t + 1) * 16, :LANES].astype(BF16))
                    left.append(part[64:, :LANES])
                    rest.append(part[:, LANES:])
            edge = jnp.where(piece < 2, jnp.where(piece < 1, rest[0], rest[1]),
                             jnp.where(piece < 3, rest[2], rest[3])).astype(BF16)
            for t in range(4):
                fours = jnp.concatenate([a[t * 4:(t + 1) * 4] for a in left], axis=0)
                made[g, b * 4 + t, pl.ds(64, 16), :] = fours.astype(BF16)
                made[g, b * 4 + t, pl.ds(80, 16), :] = edge[t * 16:(t + 1) * 16]
                made[g, b * 4 + t, pl.ds(96, 16), :] = edge[64:]

    def deliver(g, k):
        owner = flip(slot, k)
        step = 0 if DIRECTION[g] == DOWN else -1
        return pltpu.make_async_remote_copy(
            src_ref=made.at[g, owner], dst_ref=got.at[g, slot],
            send_sem=send_r.at[g, k], recv_sem=recv_r.at[g, k],
            device_id=device(plane + step, owner), device_id_type=MESH)

    def retain(g):
        return pltpu.make_async_copy(made.at[g, slot], got.at[g, slot], local.at[GROUPS + g])

    def pass_on(g):
        for k in NEAR_FIRST:
            exchange(g, k).wait_recv()
            forward(g, k).start()

    def work(g):
        keep(g).wait()
        for k in range(SLOTS):
            forward(g, k).wait_recv()
        cross(g)
        if DIRECTION[g] == DOWN:
            retain(g).start()
        for k in SEND_ORDER + ((0,) if DIRECTION[g] == UP else ()):
            deliver(g, k).start()

    for g in range(GROUPS):
        exchange(g, 1).wait_recv()
        forward(g, 1).start()
    pass_on(0)
    pass_on(1)
    def collect(g):
        retain(g).wait()
        for k in range(1, SLOTS):
            deliver(g, k).wait_recv()

        def spread(d, carry):
            row = pl.multiple_of((g * SLOTS + d) * ROWS, 16)
            gotf[pl.ds(row, ROWS), :] = got[g, d].astype(F32)
            return carry

        lax.fori_loop(0, SLOTS, spread, 0)

    pass_on(2)
    work(0)
    pass_on(3)
    work(1)
    work(2)
    collect(0)
    collect(1)
    work(3)
    collect(2)
    collect(3)

    fetch_lag.wait()
    sources = GROUPS * SLOTS
    low16 = lax.broadcasted_iota(jnp.int32, (16, LANES), 1) // 32

    def rows_of(row):
        return gotf[pl.ds(row, sources, stride=ROWS), :]

    def lags(first, row_main, row_edge, stride_ff, stride_r):
        z = jnp.concatenate([rows_of(row_edge + j) for j in range(4)], axis=0).T
        pieces = []
        for j in range(4):
            for r in range(2):
                total = None
                for ff in range(2):
                    for c in range(2):
                        at = (ff * 4 + r * 2 + c) * 16
                        to = ff * 2 + c
                        moved = z[at:at + 16]
                        if (to - j) % 4:
                            moved = pltpu.roll(moved, ((to - j) % 4) * 32, 1)
                        total = moved if total is None else jnp.where(low16 == to, moved, total)
                pieces.append(total)
        edge = jnp.dot(jnp.concatenate(pieces, axis=0).astype(BF16), lag_ref[1], preferred_element_type=F32)
        for r in range(2):
            for half in range(2):
                rows = []
                for j in (2 * half, 2 * half + 1):
                    for ff in range(2):
                        rows.append(rows_of(row_main + ff * stride_ff + r * stride_r + j))
                z = jnp.concatenate(rows, axis=0).T
                top, bottom = z[:64], z[64:]
                lhs = jnp.concatenate([jnp.where(low, top, pltpu.roll(bottom, 64, 1)),
                                       jnp.where(low, pltpu.roll(top, 64, 1), bottom)], axis=0)
                body = jnp.dot(lhs.astype(BF16), lag_ref[0], preferred_element_type=F32)
                for n in range(2):
                    j = 2 * half + n
                    at = (j * 2 + r) * 16
                    pieces = []
                    for t in range(4):
                        pieces.append(body[n * 64 + t * 16:n * 64 + (t + 1) * 16])
                        pieces.append(edge[at + t * 4:at + (t + 1) * 4])
                    out_ref[r, first + j] = jnp.concatenate(pieces, axis=0).astype(BF16)

    def lags_first(n, carry):
        lags(4 * n, 4 * n, 80 + 4 * n, 32, 16)
        return carry

    lax.fori_loop(0, 4, lags_first, 0, unroll=4)
    lags(16, 64, 96 + 4 * quarter, 8, 4)

    for g in range(GROUPS):
        for k in range(1, SLOTS):
            exchange(g, k).wait_send()
        for k in range(SLOTS):
            forward(g, k).wait_send()
        for k in range(0 if DIRECTION[g] == UP else 1, SLOTS):
            deliver(g, k).wait_send()


def shards(spectra, live_mask):
    windows = spectra.shape[0] * lax.axis_size("tm")
    tables = jnp.asarray(lag_tables(windows))
    vmem = pl.BlockSpec(memory_space=pltpu.VMEM)
    dma = pltpu.SemaphoreType.DMA
    return pl.pallas_call(
        kernel,
        out_shape=jax.ShapeDtypeStruct((2, 20, CH, LANES), BF16),
        in_specs=[pl.BlockSpec(memory_space=pltpu.HBM)] * 3,
        out_specs=vmem,
        scratch_shapes=[
            pltpu.VMEM((WIN, CH, LANES), BF16),
            pltpu.SMEM((CH,), jnp.int32),
            pltpu.VMEM((2, LANES, LANES), BF16),
            pltpu.VMEM((WIN * CH, LANES), F32),
            pltpu.VMEM((64 * CH, LANES), F32),
            pltpu.VMEM((SLOTS, GROUPS, 2, CH, LANES), BF16),
            pltpu.VMEM((GROUPS, SLOTS, 2, CH, LANES), BF16),
            pltpu.VMEM((GROUPS, SLOTS, 2, CH, LANES), BF16),
            pltpu.VMEM((GROUPS, SLOTS, ROWS, LANES), BF16),
            pltpu.VMEM((GROUPS, SLOTS, ROWS, LANES), BF16),
            pltpu.VMEM((GROUPS * SLOTS * ROWS, LANES), F32),
            dma((GROUPS, SLOTS)), dma((GROUPS, SLOTS)),
            dma((GROUPS, SLOTS)), dma((GROUPS, SLOTS)),
            dma((GROUPS, SLOTS)), dma((GROUPS, SLOTS)),
            dma((2 * GROUPS,)), dma((CH // CHUNK + 2,)),
        ],
        compiler_params=pltpu.CompilerParams(
            collective_id=0, has_side_effects=True, vmem_limit_bytes=40 * 2**20),
        name="correlate",
    )(*(pltpu.with_memory_space_constraint(a, pltpu.HBM) for a in (spectra, live_mask, tables)))


def solution(mesh):
    placed = (P("tm", "chan", None), P("chan"))
    return jax.shard_map(
        shards, mesh=mesh, in_specs=placed, out_specs=P(None, "tm", "chan", None), check_vma=False
    )
```

```python
import functools
import math

import jax
import jax.numpy as jnp
import ml_dtypes
import numpy as np
from jax import lax
from jax.experimental import pallas as pl
from jax.experimental.pallas import tpu as pltpu
from jax.sharding import PartitionSpec as P

MESH = pl.DeviceIdType.MESH
F32, BF16 = jnp.float32, jnp.bfloat16
PLANES = 64
SLOTS = 8
CH = 80
WIN = 64
LANES = 128
GROUPS = 4
ROWS = 112
DOWN, UP = 0, 1
DIRECTION = (DOWN, DOWN, DOWN, DOWN)
CHUNK = 16
NEAR_FIRST = (2, 3, 6, 7, 4, 5)
SEND_ORDER = (1, 4, 5, 6, 7, 2, 3)


def lag_tables(windows_all):
    bins = np.arange(64)
    shifts = np.arange(128) - 64
    phase = 2.0 * np.pi / 128 * bins[:, None] * shifts[None, :]
    weight = np.where(bins == 0, 1.0, 2.0)
    scaling = 1.0 / (2.0 * math.sqrt(64 * windows_all))
    parts = np.stack([weight[:, None] * np.cos(phase), -weight[:, None] * np.sin(phase)]) * scaling
    parts = parts.reshape(2, SLOTS, GROUPS, 2, LANES)
    main = parts.transpose(0, 3, 2, 1, 4).reshape(LANES, LANES)
    rest = parts.transpose(3, 0, 2, 1, 4).reshape(LANES, LANES)
    return np.stack([main, rest]).astype(ml_dtypes.bfloat16)


def flip(slot, bits):
    for bit in range(3):
        if bits >> bit & 1:
            step = 1 << bit
            slot = slot + step - 2 * step * ((slot // step) % 2)
    return slot


def device(plane, slot):
    plane = (plane + PLANES) % PLANES
    return (plane * 2 + slot // 4, slot % 4)


def kernel(x_hbm, mask_hbm, lag_hbm, out_ref, x_ref, mask_ref, lag_ref, xf, tf, sent, own, other, made, got, gotf,
           send_a, recv_a, send_z, recv_z, send_r, recv_r, local, load):
    plane = lax.axis_index("chan") // 2
    quarter = lax.axis_index("tm")
    slot = (lax.axis_index("chan") % 2) * 4 + quarter
    any_up = UP in DIRECTION

    def fetch(n):
        part = (slice(None), pl.ds(pl.multiple_of(n * CHUNK, CHUNK), CHUNK), slice(None))
        return pltpu.make_async_copy(x_hbm.at[part], x_ref.at[part], load.at[n])

    chunks = CH // CHUNK
    fetch_mask = pltpu.make_async_copy(mask_hbm, mask_ref, load.at[chunks])
    fetch_lag = pltpu.make_async_copy(lag_hbm, lag_ref, load.at[chunks + 1])
    fetch_mask.start()
    for n in range(chunks):
        fetch(n).start()
    fetch_lag.start()

    barrier = pltpu.get_barrier_semaphore()
    greeted = [device(plane, flip(slot, k)) for k in range(1, SLOTS)]
    for step in (-1, 1):
        greeted += [device(plane + step, flip(slot, k)) for k in range(SLOTS if any_up else 1)]
    for target in greeted:
        pl.semaphore_signal(barrier, inc=1, device_id=target, device_id_type=MESH)

    lane = lax.broadcasted_iota(jnp.int32, (64, LANES), 1)
    low = lane < 64

    def turn(channel):
        t, m = channel // 20, channel % 20
        place = 16 * t + m + (m // 16) * (48 - 12 * t)
        pair = [xf[pl.ds(channel + k, WIN, stride=CH), :] for k in range(2)]
        z = jnp.concatenate(pair, axis=0).astype(BF16).T.astype(F32)
        power = jnp.sum(z * z, axis=0, keepdims=True) * (1.0 / LANES)
        live0 = mask_ref[channel].astype(F32)
        live1 = mask_ref[channel + 1].astype(F32)
        z = z * (lax.rsqrt(power + 1e-6) * jnp.where(low[:1], live0, live1))
        top, bottom = z[:64], z[64:]
        tf[pl.ds(place, 64, stride=CH), :] = jnp.where(low, top, pltpu.roll(bottom, 64, 1))
        tf[pl.ds(place + 1, 64, stride=CH), :] = jnp.where(low, pltpu.roll(top, 64, 1), bottom)

    def prepare(n, carry):
        fetch(n).wait()
        first = pl.multiple_of(n * CHUNK, CHUNK)

        def widen(w, c):
            for k in range(8):
                row = pl.multiple_of((w * 8 + k) * CH + first, CHUNK)
                xf[pl.ds(row, CHUNK), :] = x_ref[w * 8 + k, pl.ds(first, CHUNK), :].astype(F32)
            return c

        lax.fori_loop(0, WIN // 8, widen, 0, unroll=4)
        for k in range(0, CHUNK, 2):
            turn(first + k)
        return carry

    fetch_mask.wait()
    lax.fori_loop(0, chunks, prepare, 0)

    def exchange(g, k):
        peer = flip(slot, k)
        return pltpu.make_async_remote_copy(
            src_ref=sent.at[peer, g], dst_ref=own.at[g, slot],
            send_sem=send_a.at[g, k], recv_sem=recv_a.at[g, k],
            device_id=device(plane, peer), device_id_type=MESH)

    def keep(g):
        return pltpu.make_async_copy(sent.at[slot, g], own.at[g, slot], local.at[g])

    def forward(g, k):
        step = -1 if DIRECTION[g] == DOWN else 1
        source = flip(slot, k)
        return pltpu.make_async_remote_copy(
            src_ref=own.at[g, source] if k else sent.at[slot, g], dst_ref=other.at[g, source],
            send_sem=send_z.at[g, k], recv_sem=recv_z.at[g, k],
            device_id=device(plane + step, slot), device_id_type=MESH)

    for g in range(GROUPS):
        def narrow(d, carry, g=g):
            for ff in range(2):
                row = pl.multiple_of((d * 8 + g * 2 + ff) * CH, 16)
                sent[d, g, ff] = tf[pl.ds(row, CH), :].astype(BF16)
            return carry

        lax.fori_loop(0, SLOTS, narrow, 0, unroll=4)
        if g == 0:
            pl.semaphore_wait(barrier, len(greeted))
        for k in SEND_ORDER:
            exchange(g, k).start()
        forward(g, 0).start()
        keep(g).start()

    sign = jnp.where(low[:1], 1.0, -1.0).astype(F32)
    piece = lax.broadcasted_iota(jnp.int32, (CH, LANES), 1) // 32

    def block(ref, g, which, ff):
        return jnp.concatenate([ref[g, which * 4 + q, ff] for q in range(4)], axis=1)

    def crossed(ref, g, which, ff):
        parts = [pltpu.roll(ref[g, which * 4 + q, ff].astype(F32), 64, 1) * sign for q in range(4)]
        return jnp.concatenate(parts, axis=1).astype(BF16)

    def cross(g):
        lower, upper = (own, other) if DIRECTION[g] == DOWN else (other, own)
        for b in range(2):
            left, rest = [], []
            for ff in range(2):
                plain, turned = block(lower, g, b, ff), crossed(lower, g, b, ff)
                tail = [plain[64:], turned[64:]]
                weights = jnp.concatenate([plain[:64], turned[:64]] + tail * 4, axis=0)
                first = block(lower, g, 1, ff) if b == 0 else block(upper, g, 0, ff)
                second = block(upper, g, b, ff)
                streamed = jnp.concatenate([first, second], axis=0)
                product = lax.dot_general(streamed, weights, (((1,), (1,)), ((), ())),
                                          preferred_element_type=F32)
                for r in range(2):
                    part = product[r * CH:(r + 1) * CH]
                    for t in range(4):
                        made[g, b * 4 + t, pl.ds(ff * 32 + r * 16, 16), :] = (
                            part[t * 16:(t + 1) * 16, :LANES].astype(BF16))
                    left.append(part[64:, :LANES])
                    rest.append(part[:, LANES:])
            edge = jnp.where(piece < 2, jnp.where(piece < 1, rest[0], rest[1]),
                             jnp.where(piece < 3, rest[2], rest[3])).astype(BF16)
            for t in range(4):
                fours = jnp.concatenate([a[t * 4:(t + 1) * 4] for a in left], axis=0)
                made[g, b * 4 + t, pl.ds(64, 16), :] = fours.astype(BF16)
                made[g, b * 4 + t, pl.ds(80, 16), :] = edge[t * 16:(t + 1) * 16]
                made[g, b * 4 + t, pl.ds(96, 16), :] = edge[64:]

    def deliver(g, k):
        owner = flip(slot, k)
        step = 0 if DIRECTION[g] == DOWN else -1
        return pltpu.make_async_remote_copy(
            src_ref=made.at[g, owner], dst_ref=got.at[g, slot],
            send_sem=send_r.at[g, k], recv_sem=recv_r.at[g, k],
            device_id=device(plane + step, owner), device_id_type=MESH)

    def retain(g):
        return pltpu.make_async_copy(made.at[g, slot], got.at[g, slot], local.at[GROUPS + g])

    def pass_on(g):
        for k in NEAR_FIRST:
            exchange(g, k).wait_recv()
            forward(g, k).start()

    def work(g):
        keep(g).wait()
        for k in range(SLOTS):
            forward(g, k).wait_recv()
        cross(g)
        if DIRECTION[g] == DOWN:
            retain(g).start()
        for k in SEND_ORDER + ((0,) if DIRECTION[g] == UP else ()):
            deliver(g, k).start()

    for g in range(GROUPS):
        exchange(g, 1).wait_recv()
        forward(g, 1).start()
    pass_on(0)
    pass_on(1)
    def collect(g):
        retain(g).wait()
        for k in range(1, SLOTS):
            deliver(g, k).wait_recv()

        def spread(d, carry):
            row = pl.multiple_of((g * SLOTS + d) * ROWS, 16)
            gotf[pl.ds(row, ROWS), :] = got[g, d].astype(F32)
            return carry

        lax.fori_loop(0, SLOTS, spread, 0, unroll=4)

    pass_on(2)
    work(0)
    pass_on(3)
    work(1)
    work(2)
    collect(0)
    collect(1)
    work(3)
    collect(2)
    collect(3)

    fetch_lag.wait()
    sources = GROUPS * SLOTS
    low16 = lax.broadcasted_iota(jnp.int32, (16, LANES), 1) // 32

    def rows_of(row):
        return gotf[pl.ds(row, sources, stride=ROWS), :]

    def lags(first, row_main, row_edge, stride_ff, stride_r):
        z = jnp.concatenate([rows_of(row_edge + j) for j in range(4)], axis=0).T
        pieces = []
        for j in range(4):
            for r in range(2):
                total = None
                for ff in range(2):
                    for c in range(2):
                        at = (ff * 4 + r * 2 + c) * 16
                        to = ff * 2 + c
                        moved = z[at:at + 16]
                        if (to - j) % 4:
                            moved = pltpu.roll(moved, ((to - j) % 4) * 32, 1)
                        total = moved if total is None else jnp.where(low16 == to, moved, total)
                pieces.append(total)
        edge = jnp.dot(jnp.concatenate(pieces, axis=0).astype(BF16), lag_ref[1], preferred_element_type=F32)
        for r in range(2):
            for half in range(2):
                rows = []
                for j in (2 * half, 2 * half + 1):
                    for ff in range(2):
                        rows.append(rows_of(row_main + ff * stride_ff + r * stride_r + j))
                z = jnp.concatenate(rows, axis=0).T
                top, bottom = z[:64], z[64:]
                lhs = jnp.concatenate([jnp.where(low, top, pltpu.roll(bottom, 64, 1)),
                                       jnp.where(low, pltpu.roll(top, 64, 1), bottom)], axis=0)
                body = jnp.dot(lhs.astype(BF16), lag_ref[0], preferred_element_type=F32)
                for n in range(2):
                    j = 2 * half + n
                    at = (j * 2 + r) * 16
                    pieces = []
                    for t in range(4):
                        pieces.append(body[n * 64 + t * 16:n * 64 + (t + 1) * 16])
                        pieces.append(edge[at + t * 4:at + (t + 1) * 4])
                    out_ref[r, first + j] = jnp.concatenate(pieces, axis=0).astype(BF16)

    def lags_first(n, carry):
        lags(4 * n, 4 * n, 80 + 4 * n, 32, 16)
        return carry

    lax.fori_loop(0, 4, lags_first, 0, unroll=4)
    lags(16, 64, 96 + 4 * quarter, 8, 4)

    for g in range(GROUPS):
        for k in range(1, SLOTS):
            exchange(g, k).wait_send()
        for k in range(SLOTS):
            forward(g, k).wait_send()
        for k in range(0 if DIRECTION[g] == UP else 1, SLOTS):
            deliver(g, k).wait_send()


def shards(spectra, live_mask):
    windows = spectra.shape[0] * lax.axis_size("tm")
    tables = jnp.asarray(lag_tables(windows))
    vmem = pl.BlockSpec(memory_space=pltpu.VMEM)
    dma = pltpu.SemaphoreType.DMA
    return pl.pallas_call(
        kernel,
        out_shape=jax.ShapeDtypeStruct((2, 20, CH, LANES), BF16),
        in_specs=[pl.BlockSpec(memory_space=pltpu.HBM)] * 3,
        out_specs=vmem,
        scratch_shapes=[
            pltpu.VMEM((WIN, CH, LANES), BF16),
            pltpu.SMEM((CH,), jnp.int32),
            pltpu.VMEM((2, LANES, LANES), BF16),
            pltpu.VMEM((WIN * CH, LANES), F32),
            pltpu.VMEM((64 * CH, LANES), F32),
            pltpu.VMEM((SLOTS, GROUPS, 2, CH, LANES), BF16),
            pltpu.VMEM((GROUPS, SLOTS, 2, CH, LANES), BF16),
            pltpu.VMEM((GROUPS, SLOTS, 2, CH, LANES), BF16),
            pltpu.VMEM((GROUPS, SLOTS, ROWS, LANES), BF16),
            pltpu.VMEM((GROUPS, SLOTS, ROWS, LANES), BF16),
            pltpu.VMEM((GROUPS * SLOTS * ROWS, LANES), F32),
            dma((GROUPS, SLOTS)), dma((GROUPS, SLOTS)),
            dma((GROUPS, SLOTS)), dma((GROUPS, SLOTS)),
            dma((GROUPS, SLOTS)), dma((GROUPS, SLOTS)),
            dma((2 * GROUPS,)), dma((CH // CHUNK + 2,)),
        ],
        compiler_params=pltpu.CompilerParams(
            collective_id=0, has_side_effects=True, vmem_limit_bytes=40 * 2**20),
        name="correlate",
    )(*(pltpu.with_memory_space_constraint(a, pltpu.HBM) for a in (spectra, live_mask, tables)))


def solution(mesh):
    placed = (P("tm", "chan", None), P("chan"))
    return jax.shard_map(
        shards, mesh=mesh, in_specs=placed, out_specs=P(None, "tm", "chan", None), check_vma=False
    )
```
